32 devices in a mesh: expert: 8 (over z, y), replica: 4 (over x, core).
Axes of the slice: x: 2, y: 2, z: 4, core: 2. Of those that a mesh axis runs over, the one named last changes fastest.
Arguments:
- tokens: bfloat16 [8192, 7168], P(('expert', 'replica')), may hold values from -6 to 6
- routes: int32 [8192, 8], P(('expert', 'replica')), may hold values from 0 to 255, all different within a row
- counts: int32 [32], P(('expert', 'replica')), may hold values from 128 to 256, as said below
- w_gate: bfloat16 [8, 7168, 2048], P('expert', None, 'replica'), may hold values from -0.0625 to 0.0625
- w_up: bfloat16 [8, 7168, 2048], P('expert', None, 'replica'), may hold values from -0.0625 to 0.0625
Outputs:
- key_cov: float32 [8, 2048, 2048], P('expert', 'replica')
The draws below stay inside these ranges and needn't reach their ends.
Inputs may be any that keep to these rules, and one draw needn't show every extreme that they name: `counts`: every count is a multiple of 128; some device has 256 and some 128.
All inputs are finite; a program needn't handle non-finite values.
Results may differ from the reference program's by a relative error of at most 0.0039.
Values may be sent and summed in bfloat16 or wider, within the bound.
A program may use at most 128 MiB of HBM per device.

```python
import jax
import jax.numpy as jnp
from jax import lax

D = 7168
FF = 2048
N_ROUTED = 256
TOP = 8
TOK_DEV = 256
TOKENS = 8192
EXPERTS = 8
CAP = 8
SLOTS = 64
N_EXPERT = 8
N_REPLICA = 4


def draw_counts(key, part):
    device_total = N_EXPERT * N_REPLICA
    block_total = TOK_DEV // 128
    first_key, second_key = jax.random.split(jax.random.fold_in(key, 17))
    values = jax.random.randint(first_key, (device_total,), 1, block_total + 1) * 128
    chosen = jax.random.randint(second_key, (), 0, device_total)
    position = jnp.arange(device_total)
    values = jnp.where(position == chosen, TOK_DEV, values)
    values = jnp.where(position == (chosen + 1) % device_total, 128, values)
    return values.astype(jnp.int32)


def block_scale(own_key, shape, cuts, low, high):
    def one(dim, parts):
        draws = jax.random.uniform(jax.random.fold_in(jax.random.fold_in(own_key, 6), dim), (parts,), jnp.float32, low / len(cuts), high / len(cuts))
        return jnp.repeat(jnp.exp(draws), shape[dim] // parts).reshape((-1,) + (1,) * (len(shape) - dim - 1))

    loudness = one(*cuts[0])
    for cut in cuts[1:]:
        loudness = loudness * one(*cut)
    return loudness


def choose_distinct(key, rows, number_of, top, lift):
    sequence = jax.random.permutation(jax.random.fold_in(key, 1), number_of)
    pull = sequence
    for power in range(3):
        pull = pull * pull // number_of
    pull = pull * lift // number_of
    lots = jax.random.randint(jax.random.fold_in(key, 2), (rows, number_of), 0, 4096) + pull
    sure = jax.random.permutation(jax.random.fold_in(key, 3), rows)[jnp.arange(number_of) % rows]
    lots = jnp.where(jnp.arange(rows)[:, None] == sure[None, :], 1 << 14, lots)
    score = lots * number_of + jnp.arange(number_of)
    return lax.top_k(score.astype(jnp.int32), top)[1].astype(jnp.int32)


def normal_values(own_key, extent, spread, limit, shards=(), kind=jnp.bfloat16):
    drawn = jax.random.normal(own_key, extent, jnp.float32) * spread
    if len(shards) > 0:
        drawn = block_scale(own_key, extent, shards, -0.22, 0.18) * drawn
    return jnp.clip(drawn, min=-limit, max=limit).astype(kind)


def setup_inputs(seed: int = 0) -> dict:
    seeds = jax.random.split(jax.random.key(seed), 6)
    return {
        "tokens": normal_values(seeds[0], (TOKENS, D), 1.0, 6.0, ((0, 32),)),
        "routes": choose_distinct(seeds[1], TOKENS, N_ROUTED, TOP, 512),
        "counts": draw_counts(jax.random.fold_in(seeds[5], 71), 0),
        "w_gate": normal_values(seeds[3], (EXPERTS, D, FF), D ** -0.5, 0.0625, ((0, 8), (2, 4))),
        "w_up": normal_values(seeds[4], (EXPERTS, D, FF), D ** -0.5, 0.0625, ((0, 8), (2, 4))),
    }


def slot_tokens(route_block, real_count, expert_total, capacity):
    flat_route = route_block.reshape(-1)
    position = jnp.arange(flat_route.shape[0], dtype=jnp.int32)
    owner_token = position // TOP
    usable = (owner_token < real_count) & (flat_route < expert_total)
    hit_table = ((flat_route[:, None] == jnp.arange(expert_total, dtype=jnp.int32)[None, :]) & usable[:, None]).astype(jnp.int32)
    slot_rank = jnp.sum((jnp.cumsum(hit_table, axis=0) - hit_table) * hit_table, axis=1)
    kept_slot = usable & (slot_rank < capacity)
    slot_index = flat_route * capacity + slot_rank
    slot_match = kept_slot[:, None] & (slot_index[:, None] == jnp.arange(expert_total * capacity, dtype=jnp.int32)[None, :])
    filled = jnp.any(slot_match, axis=0)
    source = jnp.sum(jnp.where(slot_match, owner_token[:, None], 0), axis=0).astype(jnp.int32)
    return source, filled


def reference(tokens, routes, counts, w_gate, w_up):
    device_total = N_EXPERT * N_REPLICA
    route_blocks = routes.reshape(device_total, TOK_DEV, TOP)

    def per_device(items):
        return slot_tokens(items[0], items[1], EXPERTS, CAP)

    source, filled = lax.map(per_device, (route_blocks, counts))
    shifted = source + (jnp.arange(device_total, dtype=jnp.int32) * TOK_DEV)[:, None]
    row_index = shifted.reshape(device_total, EXPERTS, CAP).transpose(1, 0, 2).reshape(EXPERTS, device_total * CAP).astype(jnp.int32)
    row_live = filled.reshape(device_total, EXPERTS, CAP).transpose(1, 0, 2).reshape(EXPERTS, device_total * CAP)
    factor = 1.0 / SLOTS

    def per_expert(items):
        index_rows, live_rows, gate_matrix, up_matrix = items
        slot_rows = jnp.where(live_rows[:, None], tokens[index_rows], jnp.zeros((), tokens.dtype))
        gate_pre = jnp.dot(slot_rows, gate_matrix, preferred_element_type=jnp.float32)
        up_pre = jnp.dot(slot_rows, up_matrix, preferred_element_type=jnp.float32)
        keys = (jax.nn.silu(gate_pre) * up_pre).astype(jnp.bfloat16)
        return jnp.einsum("rf,rg->fg", keys, keys, preferred_element_type=jnp.float32) * factor

    return lax.map(per_expert, (row_index, row_live, w_gate, w_up))
```

```python
import functools

import jax
import jax.numpy as jnp
from jax import lax
from jax.experimental import pallas as pl
from jax.experimental.pallas import tpu as pltpu
from jax.sharding import PartitionSpec as P

N_ROUTED = 256
TOP = 8
MESH = pl.DeviceIdType.MESH


def exchange_kernel(
    sizes, counts_ref, routes_ref, tokens_hbm, gate_hbm, up_hbm, keys_ref, own_ref,
    tok, wg, wu, slots, rows, acc_g, acc_u, kbuf,
    tok_sem, wg_sem, wu_sem, a_send, a_recv, x_send, x_recv, s_send, s_recv,
    f_send, f_recv, k_send, k_recv,
):
    n_e, n_r, cap, n_tok, n_k, kc, pieces = sizes
    total_rows = n_e * n_r * cap
    piece = total_rows // pieces
    hidden = acc_g.shape[1]
    e = lax.axis_index("expert")
    r = lax.axis_index("replica")
    sib = r + 1 - 2 * (r % 2)
    across = (r + 2) % n_r

    def tok_copy(k):
        return pltpu.make_async_copy(
            tokens_hbm.at[:, pl.ds(k * kc, kc)], tok.at[k], tok_sem.at[k])

    def w_copy(hbm, buf, sem, k):
        return pltpu.make_async_copy(hbm.at[0, pl.ds(k * kc, kc), :], buf.at[k], sem.at[k])

    barrier = pltpu.get_barrier_semaphore()
    for s in range(1, n_e):
        pl.semaphore_signal(barrier, inc=1, device_id=((e + s) % n_e, r), device_id_type=MESH)
    pl.semaphore_signal(barrier, inc=1, device_id=(e, sib), device_id_type=MESH)
    pl.semaphore_signal(barrier, inc=1, device_id=(e, across), device_id_type=MESH)

    for k in range(n_k):
        tok_copy(k).start()
    for k in range(n_k):
        w_copy(gate_hbm, wg, wg_sem, k).start()
        w_copy(up_hbm, wu, wu_sem, k).start()

    n_s = n_e * cap
    count = counts_ref[0]
    slot = lax.broadcasted_iota(jnp.int32, (n_s, n_tok), 0)
    token = lax.broadcasted_iota(jnp.int32, (n_s, n_tok), 1)
    slot_expert = slot // cap
    hit = routes_ref[0:1, :] == slot_expert
    for c in range(1, TOP):
        hit = hit | (routes_ref[c:c + 1, :] == slot_expert)
    hit = hit & (token < count)
    before = lax.broadcasted_iota(jnp.int32, (n_tok, n_tok), 0) < lax.broadcasted_iota(
        jnp.int32, (n_tok, n_tok), 1)
    hit_f = jnp.where(hit, 1.0, 0.0)
    rank = jnp.dot(
        hit_f.astype(jnp.bfloat16), jnp.where(before, 1.0, 0.0).astype(jnp.bfloat16),
        preferred_element_type=jnp.float32)
    place = (slot % cap).astype(jnp.float32)
    choice = jnp.where(rank == place, hit_f, 0.0).astype(jnp.bfloat16)

    acc_g[...] = jnp.zeros_like(acc_g)
    acc_u[...] = jnp.zeros_like(acc_u)

    pl.semaphore_wait(barrier, n_e + 1)

    def a_copy(k, s):
        return pltpu.make_async_remote_copy(
            src_ref=slots.at[k, (e + s) % n_e], dst_ref=rows.at[k, r, e],
            send_sem=a_send.at[k, s], recv_sem=a_recv.at[k, s],
            device_id=((e + s) % n_e, r), device_id_type=MESH)

    def row_copy(k, who, to, send, recv):
        return pltpu.make_async_remote_copy(
            src_ref=rows.at[k, who], dst_ref=rows.at[k, who],
            send_sem=send.at[k], recv_sem=recv.at[k],
            device_id=(e, to), device_id_type=MESH)

    def x_copy(k):
        return row_copy(k, r, across, x_send, x_recv)

    def s_copy(k):
        return row_copy(k, r, sib, s_send, s_recv)

    def f_copy(k):
        return row_copy(k, across, sib, f_send, f_recv)

    half = n_e // 2
    order = sorted(range(1, n_e), key=lambda s: abs(s - half))

    @pl.loop(0, n_k)
    def _(k):
        tok_copy(k).wait()
        picked = jnp.dot(choice, tok[k], preferred_element_type=jnp.float32)
        slots[k] = picked.reshape(n_e, cap, kc).astype(jnp.bfloat16)
        for s in order:
            a_copy(k, s).start()
        rows[k, r, e] = slots[k, e]

    groups = max(1, total_rows // 256)
    per = n_r // groups
    step_rows = total_rows // groups

    @pl.loop(0, n_k + 2)
    def _(i):
        @pl.when(i < n_k)
        def _():
            for s in order:
                a_copy(i, s).wait_recv()
            x_copy(i).start()
            s_copy(i).start()

        @pl.when((i >= 1) & (i <= n_k))
        def _():
            x_copy(i - 1).wait_recv()
            f_copy(i - 1).start()

        @pl.when(i >= 2)
        def _():
            k = i - 2
            w_copy(gate_hbm, wg, wg_sem, k).wait()
            w_copy(up_hbm, wu, wu_sem, k).wait()
            s_copy(k).wait_recv()
            f_copy(k).wait_recv()
            for g in range(groups):
                block = rows[k, g * per:(g + 1) * per].reshape(step_rows, kc)
                at = slice(g * step_rows, (g + 1) * step_rows)
                acc_g[at, :] += jnp.dot(block, wg[k], preferred_element_type=jnp.float32)
                acc_u[at, :] += jnp.dot(block, wu[k], preferred_element_type=jnp.float32)

    def key_copy(p, who, to, n):
        return pltpu.make_async_remote_copy(
            src_ref=kbuf.at[p, who], dst_ref=kbuf.at[p, who],
            send_sem=k_send.at[n, p], recv_sem=k_recv.at[n, p],
            device_id=(e, to), device_id_type=MESH)

    for p in range(pieces):
        g = acc_g[p * piece:(p + 1) * piece, :]
        u = acc_u[p * piece:(p + 1) * piece, :]
        key = ((g / (1.0 + jnp.exp(-g))) * u).astype(jnp.bfloat16)
        kbuf[p, r] = key
        own_ref[p * piece:(p + 1) * piece, :] = key
        key_copy(p, r, across, 0).start()
        key_copy(p, r, sib, 1).start()
    for p in range(pieces):
        key_copy(p, r, across, 0).wait_recv()
        key_copy(p, across, sib, 2).start()
    for p in range(pieces):
        key_copy(p, r, sib, 1).wait_recv()
        key_copy(p, across, sib, 2).wait_recv()
        for q in range(n_r):
            keys_ref[p * piece:(p + 1) * piece, q * hidden:(q + 1) * hidden] = kbuf[p, q]

    @pl.loop(0, n_k)
    def _(k):
        for s in order:
            a_copy(k, s).wait_send()
        x_copy(k).wait_send()
        s_copy(k).wait_send()
        f_copy(k).wait_send()

    for p in range(pieces):
        key_copy(p, r, across, 0).wait_send()
        key_copy(p, r, sib, 1).wait_send()
        key_copy(p, across, sib, 2).wait_send()


def body(tokens, routes, counts, w_gate, w_up):
    n_e = lax.axis_size("expert")
    n_r = lax.axis_size("replica")
    n_tok, width = tokens.shape
    hidden = w_gate.shape[2]
    cap = n_tok * TOP // N_ROUTED
    n_k = 7
    kc = width // n_k
    pieces = 4
    total = n_e * n_r * cap
    sizes = (n_e, n_r, cap, n_tok, n_k, kc, pieces)
    bf = jnp.bfloat16
    dma = pltpu.SemaphoreType.DMA
    vmem = pl.BlockSpec(memory_space=pltpu.VMEM)
    hbm = pl.BlockSpec(memory_space=pl.ANY)
    keys, own = pl.pallas_call(
        functools.partial(exchange_kernel, sizes),
        out_shape=(
            jax.ShapeDtypeStruct((total, n_r * hidden), bf),
            jax.ShapeDtypeStruct((total, hidden), bf),
        ),
        in_specs=[pl.BlockSpec(memory_space=pltpu.SMEM), vmem, hbm, hbm, hbm],
        out_specs=(vmem, vmem),
        scratch_shapes=[
            pltpu.VMEM((n_k, n_tok, kc), bf),
            pltpu.VMEM((n_k, kc, hidden), bf),
            pltpu.VMEM((n_k, kc, hidden), bf),
            pltpu.VMEM((n_k, n_e, cap, kc), bf),
            pltpu.VMEM((n_k, n_r, n_e, cap, kc), bf),
            pltpu.VMEM((total, hidden), jnp.float32),
            pltpu.VMEM((total, hidden), jnp.float32),
            pltpu.VMEM((pieces, n_r, total // pieces, hidden), bf),
            dma((n_k,)), dma((n_k,)), dma((n_k,)),
            dma((n_k, n_e)), dma((n_k, n_e)),
            dma((n_k,)), dma((n_k,)), dma((n_k,)), dma((n_k,)), dma((n_k,)), dma((n_k,)),
            dma((3, pieces)), dma((3, pieces)),
        ],
        compiler_params=pltpu.CompilerParams(
            collective_id=0, has_side_effects=True, vmem_limit_bytes=60 * 1024 * 1024),
        cost_estimate=pl.CostEstimate(
            flops=4 * total * width * hidden,
            bytes_accessed=4 * width * hidden + 2 * n_tok * width,
            transcendentals=total * hidden),
    )(counts, routes.T, tokens, w_gate, w_up)
    factor = 1.0 / (n_e * cap)
    gram = jnp.einsum("rf,rg->fg", own, keys, preferred_element_type=jnp.float32) * factor
    return gram[None]


def solution(mesh):
    return jax.shard_map(
        body,
        mesh=mesh,
        in_specs=(
            P(("expert", "replica"), None),
            P(("expert", "replica"), None),
            P(("expert", "replica")),
            P("expert", None, "replica"),
            P("expert", None, "replica"),
        ),
        out_specs=P("expert", "replica", None),
        check_vma=False,
    )
```

```python
import functools

import jax
import jax.numpy as jnp
from jax import lax
from jax.experimental import pallas as pl
from jax.experimental.pallas import tpu as pltpu
from jax.sharding import PartitionSpec as P

N_ROUTED = 256
TOP = 8
MESH = pl.DeviceIdType.MESH


def exchange_kernel(
    sizes, counts_ref, routes_ref, tokens_hbm, gate_hbm, up_hbm, keys_ref, own_ref,
    tok, wg, wu, slots, rows, acc_g, acc_u, kbuf,
    tok_sem, wg_sem, wu_sem, a_send, a_recv, x_send, x_recv, s_send, s_recv,
    f_send, f_recv, k_send, k_recv,
):
    n_e, n_r, cap, n_tok, n_k, kc, pieces = sizes
    total_rows = n_e * n_r * cap
    piece = total_rows // pieces
    hidden = acc_g.shape[1]
    e = lax.axis_index("expert")
    r = lax.axis_index("replica")
    sib = r + 1 - 2 * (r % 2)
    across = (r + 2) % n_r

    def tok_copy(k):
        return pltpu.make_async_copy(
            tokens_hbm.at[:, pl.ds(k * kc, kc)], tok.at[k], tok_sem.at[k])

    def w_copy(hbm, buf, sem, k):
        return pltpu.make_async_copy(hbm.at[0, pl.ds(k * kc, kc), :], buf.at[k], sem.at[k])

    barrier = pltpu.get_barrier_semaphore()
    for s in range(1, n_e):
        pl.semaphore_signal(barrier, inc=1, device_id=((e + s) % n_e, r), device_id_type=MESH)
    pl.semaphore_signal(barrier, inc=1, device_id=(e, sib), device_id_type=MESH)
    pl.semaphore_signal(barrier, inc=1, device_id=(e, across), device_id_type=MESH)

    for k in range(n_k):
        tok_copy(k).start()
    for k in range(n_k):
        w_copy(gate_hbm, wg, wg_sem, k).start()
        w_copy(up_hbm, wu, wu_sem, k).start()

    n_s = n_e * cap
    count = counts_ref[0]
    slot = lax.broadcasted_iota(jnp.int32, (n_s, n_tok), 0)
    token = lax.broadcasted_iota(jnp.int32, (n_s, n_tok), 1)
    slot_expert = slot // cap
    hit = routes_ref[0:1, :] == slot_expert
    for c in range(1, TOP):
        hit = hit | (routes_ref[c:c + 1, :] == slot_expert)
    hit = hit & (token < count)
    before = lax.broadcasted_iota(jnp.int32, (n_tok, n_tok), 0) < lax.broadcasted_iota(
        jnp.int32, (n_tok, n_tok), 1)
    hit_f = jnp.where(hit, 1.0, 0.0)
    rank = jnp.dot(
        hit_f.astype(jnp.bfloat16), jnp.where(before, 1.0, 0.0).astype(jnp.bfloat16),
        preferred_element_type=jnp.float32)
    place = (slot % cap).astype(jnp.float32)
    choice = jnp.where(rank == place, hit_f, 0.0).astype(jnp.bfloat16)

    acc_g[...] = jnp.zeros_like(acc_g)
    acc_u[...] = jnp.zeros_like(acc_u)

    pl.semaphore_wait(barrier, n_e + 1)

    def a_copy(k, s):
        return pltpu.make_async_remote_copy(
            src_ref=slots.at[k, (e + s) % n_e], dst_ref=rows.at[k, r, e],
            send_sem=a_send.at[k, s], recv_sem=a_recv.at[k, s],
            device_id=((e + s) % n_e, r), device_id_type=MESH)

    def row_copy(k, who, to, send, recv):
        return pltpu.make_async_remote_copy(
            src_ref=rows.at[k, who], dst_ref=rows.at[k, who],
            send_sem=send.at[k], recv_sem=recv.at[k],
            device_id=(e, to), device_id_type=MESH)

    def x_copy(k):
        return row_copy(k, r, across, x_send, x_recv)

    def s_copy(k):
        return row_copy(k, r, sib, s_send, s_recv)

    def f_copy(k):
        return row_copy(k, across, sib, f_send, f_recv)

    half = n_e // 2
    order = sorted(range(1, n_e), key=lambda s: abs(s - half))

    groups = max(1, total_rows // 256)
    per = n_r // groups
    step_rows = total_rows // groups
    ahead, lag_x, lag_f = 3, 2, 1
    at_x = ahead + lag_x
    at_f = at_x + lag_f

    @pl.loop(0, n_k + at_f)
    def _(i):
        @pl.when(i < n_k)
        def _():
            tok_copy(i).wait()
            picked = jnp.dot(choice, tok[i], preferred_element_type=jnp.float32)
            slots[i] = picked.reshape(n_e, cap, kc).astype(jnp.bfloat16)
            for s in order:
                a_copy(i, s).start()
            rows[i, r, e] = slots[i, e]

        @pl.when((i >= ahead) & (i < n_k + ahead))
        def _():
            k = i - ahead
            for s in order:
                a_copy(k, s).wait_recv()
            x_copy(k).start()
            s_copy(k).start()

        @pl.when((i >= at_x) & (i < n_k + at_x))
        def _():
            k = i - at_x
            x_copy(k).wait_recv()
            f_copy(k).start()

        @pl.when(i >= at_f)
        def _():
            k = i - at_f
            w_copy(gate_hbm, wg, wg_sem, k).wait()
            w_copy(up_hbm, wu, wu_sem, k).wait()
            s_copy(k).wait_recv()
            f_copy(k).wait_recv()
            for g in range(groups):
                block = rows[k, g * per:(g + 1) * per].reshape(step_rows, kc)
                at = slice(g * step_rows, (g + 1) * step_rows)
                acc_g[at, :] += jnp.dot(block, wg[k], preferred_element_type=jnp.float32)
                acc_u[at, :] += jnp.dot(block, wu[k], preferred_element_type=jnp.float32)

    def key_copy(p, who, to, n):
        return pltpu.make_async_remote_copy(
            src_ref=kbuf.at[p, who], dst_ref=kbuf.at[p, who],
            send_sem=k_send.at[n, p], recv_sem=k_recv.at[n, p],
            device_id=(e, to), device_id_type=MESH)

    for p in range(pieces):
        g = acc_g[p * piece:(p + 1) * piece, :]
        u = acc_u[p * piece:(p + 1) * piece, :]
        key = ((g / (1.0 + jnp.exp(-g))) * u).astype(jnp.bfloat16)
        kbuf[p, r] = key
        key_copy(p, r, across, 0).start()
        key_copy(p, r, sib, 1).start()
    own_ref[...] = kbuf[:, r].reshape(total_rows, hidden).T
    for p in range(pieces):
        key_copy(p, r, across, 0).wait_recv()
        key_copy(p, across, sib, 2).start()
    for p in range(pieces):
        key_copy(p, r, sib, 1).wait_recv()
        key_copy(p, across, sib, 2).wait_recv()
        for q in range(n_r):
            keys_ref[p * piece:(p + 1) * piece, q * hidden:(q + 1) * hidden] = kbuf[p, q]

    @pl.loop(0, n_k)
    def _(k):
        for s in order:
            a_copy(k, s).wait_send()
        x_copy(k).wait_send()
        s_copy(k).wait_send()
        f_copy(k).wait_send()

    for p in range(pieces):
        key_copy(p, r, across, 0).wait_send()
        key_copy(p, r, sib, 1).wait_send()
        key_copy(p, across, sib, 2).wait_send()


def body(tokens, routes, counts, w_gate, w_up):
    n_e = lax.axis_size("expert")
    n_r = lax.axis_size("replica")
    n_tok, width = tokens.shape
    hidden = w_gate.shape[2]
    cap = n_tok * TOP // N_ROUTED
    n_k = 14
    kc = width // n_k
    pieces = 4
    total = n_e * n_r * cap
    sizes = (n_e, n_r, cap, n_tok, n_k, kc, pieces)
    bf = jnp.bfloat16
    dma = pltpu.SemaphoreType.DMA
    vmem = pl.BlockSpec(memory_space=pltpu.VMEM)
    hbm = pl.BlockSpec(memory_space=pl.ANY)
    keys, own = pl.pallas_call(
        functools.partial(exchange_kernel, sizes),
        out_shape=(
            jax.ShapeDtypeStruct((total, n_r * hidden), bf),
            jax.ShapeDtypeStruct((hidden, total), bf),
        ),
        in_specs=[pl.BlockSpec(memory_space=pltpu.SMEM), vmem, hbm, hbm, hbm],
        out_specs=(vmem, vmem),
        scratch_shapes=[
            pltpu.VMEM((n_k, n_tok, kc), bf),
            pltpu.VMEM((n_k, kc, hidden), bf),
            pltpu.VMEM((n_k, kc, hidden), bf),
            pltpu.VMEM((n_k, n_e, cap, kc), bf),
            pltpu.VMEM((n_k, n_r, n_e, cap, kc), bf),
            pltpu.VMEM((total, hidden), jnp.float32),
            pltpu.VMEM((total, hidden), jnp.float32),
            pltpu.VMEM((pieces, n_r, total // pieces, hidden), bf),
            dma((n_k,)), dma((n_k,)), dma((n_k,)),
            dma((n_k, n_e)), dma((n_k, n_e)),
            dma((n_k,)), dma((n_k,)), dma((n_k,)), dma((n_k,)), dma((n_k,)), dma((n_k,)),
            dma((3, pieces)), dma((3, pieces)),
        ],
        compiler_params=pltpu.CompilerParams(
            collective_id=0, has_side_effects=True, vmem_limit_bytes=60 * 1024 * 1024),
        cost_estimate=pl.CostEstimate(
            flops=4 * total * width * hidden,
            bytes_accessed=4 * width * hidden + 2 * n_tok * width,
            transcendentals=total * hidden),
    )(counts, routes.T, tokens, w_gate, w_up)
    factor = 1.0 / (n_e * cap)
    gram = jnp.einsum("fr,rg->fg", own, keys, preferred_element_type=jnp.float32) * factor
    return gram[None]


def solution(mesh):
    return jax.shard_map(
        body,
        mesh=mesh,
        in_specs=(
            P(("expert", "replica"), None),
            P(("expert", "replica"), None),
            P(("expert", "replica")),
            P("expert", None, "replica"),
            P("expert", None, "replica"),
        ),
        out_specs=P("expert", "replica", None),
        check_vma=False,
    )
```

```python
import functools

import jax
import jax.numpy as jnp
from jax import lax
from jax.experimental import pallas as pl
from jax.experimental.pallas import tpu as pltpu
from jax.sharding import PartitionSpec as P

N_ROUTED = 256
TOP = 8
MESH = pl.DeviceIdType.MESH


def exchange_kernel(
    sizes, counts_ref, routes_ref, tokens_hbm, gate_hbm, up_hbm, keys_ref, own_ref,
    tok, wg, wu, slots, rows, acc_g, acc_u, kbuf,
    tok_sem, wg_sem, wu_sem, a_send, a_recv, x_send, x_recv, s_send, s_recv,
    f_send, f_recv, k_send, k_recv,
):
    n_e, n_r, cap, n_tok, n_k, kc, pieces = sizes
    total_rows = n_e * n_r * cap
    piece = total_rows // pieces
    half_rows = total_rows // 2
    half = n_e // 2
    n_j = 2 * n_k
    hidden = acc_g.shape[1]
    e = lax.axis_index("expert")
    r = lax.axis_index("replica")
    sib = r + 1 - 2 * (r % 2)
    across = (r + 2) % n_r

    def tok_copy(k):
        return pltpu.make_async_copy(
            tokens_hbm.at[:, pl.ds(k * kc, kc)], tok.at[k], tok_sem.at[k])

    def w_copy(hbm, buf, sem, k):
        return pltpu.make_async_copy(hbm.at[0, pl.ds(k * kc, kc), :], buf.at[k], sem.at[k])

    barrier = pltpu.get_barrier_semaphore()
    for s in range(1, n_e):
        pl.semaphore_signal(barrier, inc=1, device_id=((e + s) % n_e, r), device_id_type=MESH)
    pl.semaphore_signal(barrier, inc=1, device_id=(e, sib), device_id_type=MESH)
    pl.semaphore_signal(barrier, inc=1, device_id=(e, across), device_id_type=MESH)

    for k in range(n_k):
        tok_copy(k).start()
    for k in range(n_k):
        w_copy(gate_hbm, wg, wg_sem, k).start()
        w_copy(up_hbm, wu, wu_sem, k).start()

    n_s = n_e * cap
    count = counts_ref[0]
    slot = lax.broadcasted_iota(jnp.int32, (n_s, n_tok), 0)
    token = lax.broadcasted_iota(jnp.int32, (n_s, n_tok), 1)
    slot_expert = slot // cap
    hit = routes_ref[0:1, :] == slot_expert
    for c in range(1, TOP):
        hit = hit | (routes_ref[c:c + 1, :] == slot_expert)
    hit = hit & (token < count)
    before = lax.broadcasted_iota(jnp.int32, (n_tok, n_tok), 0) < lax.broadcasted_iota(
        jnp.int32, (n_tok, n_tok), 1)
    hit_f = jnp.where(hit, 1.0, 0.0)
    rank = jnp.dot(
        hit_f.astype(jnp.bfloat16), jnp.where(before, 1.0, 0.0).astype(jnp.bfloat16),
        preferred_element_type=jnp.float32)
    place = (slot % cap).astype(jnp.float32)
    choice = jnp.where(rank == place, hit_f, 0.0).astype(jnp.bfloat16)

    acc_g[...] = jnp.zeros_like(acc_g)
    acc_u[...] = jnp.zeros_like(acc_u)

    pl.semaphore_wait(barrier, n_e + 1)

    def a_copy(j, pos):
        to = (e + 2 * pos + j // n_k) % n_e
        return pltpu.make_async_remote_copy(
            src_ref=slots.at[j % n_k, to], dst_ref=rows.at[j, r, pos],
            send_sem=a_send.at[j, pos], recv_sem=a_recv.at[j, pos],
            device_id=(to, r), device_id_type=MESH)

    def row_copy(k, who, to, send, recv):
        return pltpu.make_async_remote_copy(
            src_ref=rows.at[k, who], dst_ref=rows.at[k, who],
            send_sem=send.at[k], recv_sem=recv.at[k],
            device_id=(e, to), device_id_type=MESH)

    def x_copy(k):
        return row_copy(k, r, across, x_send, x_recv)

    def s_copy(k):
        return row_copy(k, r, sib, s_send, s_recv)

    def f_copy(k):
        return row_copy(k, across, sib, f_send, f_recv)

    order = sorted(range(half), key=lambda pos: abs(2 * pos - half))
    remote = [pos for pos in order if pos > 0]

    def key_copy(p, who, to, n):
        return pltpu.make_async_remote_copy(
            src_ref=kbuf.at[p, who], dst_ref=kbuf.at[p, who],
            send_sem=k_send.at[n, p], recv_sem=k_recv.at[n, p],
            device_id=(e, to), device_id_type=MESH)

    def finish_keys(h):
        for q in range(pieces // 2):
            p = h * (pieces // 2) + q
            g = acc_g[q * piece:(q + 1) * piece, :]
            u = acc_u[q * piece:(q + 1) * piece, :]
            kbuf[p, r] = ((g / (1.0 + jnp.exp(-g))) * u).astype(jnp.bfloat16)
            key_copy(p, r, across, 0).start()
            key_copy(p, r, sib, 1).start()

    def relay_keys(h):
        for q in range(pieces // 2):
            p = h * (pieces // 2) + q
            key_copy(p, r, across, 0).wait_recv()
            key_copy(p, across, sib, 2).start()

    def place_keys(h):
        for q in range(pieces // 2):
            p = h * (pieces // 2) + q
            key_copy(p, r, sib, 1).wait_recv()
            key_copy(p, across, sib, 2).wait_recv()
            for o in range(n_r):
                keys_ref[p * piece:(p + 1) * piece, o * hidden:(o + 1) * hidden] = kbuf[p, o]

    groups = max(1, half_rows // 256)
    per = n_r // groups
    step_rows = half_rows // groups
    ahead, lag_x, lag_f = 3, 2, 1
    at_x = ahead + lag_x
    at_f = at_x + lag_f

    @pl.loop(0, n_j + at_f)
    def _(i):
        @pl.when(i < n_k)
        def _():
            tok_copy(i).wait()
            picked = jnp.dot(choice, tok[i], preferred_element_type=jnp.float32)
            slots[i] = picked.reshape(n_e, cap, kc).astype(jnp.bfloat16)
            for pos in remote:
                a_copy(i, pos).start()
            rows[i, r, 0] = slots[i, e]

        @pl.when((i >= n_k) & (i < n_j))
        def _():
            for pos in order:
                a_copy(i, pos).start()

        @pl.when((i >= ahead) & (i < n_j + ahead))
        def _():
            j = i - ahead
            for pos in remote:
                a_copy(j, pos).wait_recv()

            @pl.when(j >= n_k)
            def _():
                a_copy(j, 0).wait_recv()

            x_copy(j).start()
            s_copy(j).start()

        @pl.when((i >= at_x) & (i < n_j + at_x))
        def _():
            j = i - at_x
            x_copy(j).wait_recv()
            f_copy(j).start()

        @pl.when(i >= at_f)
        def _():
            j = i - at_f
            k = j % n_k

            @pl.when(j < n_k)
            def _():
                w_copy(gate_hbm, wg, wg_sem, k).wait()
                w_copy(up_hbm, wu, wu_sem, k).wait()

            s_copy(j).wait_recv()
            f_copy(j).wait_recv()
            for g in range(groups):
                block = rows[j, g * per:(g + 1) * per].reshape(step_rows, kc)
                at = slice(g * step_rows, (g + 1) * step_rows)
                acc_g[at, :] += jnp.dot(block, wg[k], preferred_element_type=jnp.float32)
                acc_u[at, :] += jnp.dot(block, wu[k], preferred_element_type=jnp.float32)

        @pl.when(i == at_f + n_k - 1)
        def _():
            finish_keys(0)
            acc_g[...] = jnp.zeros_like(acc_g)
            acc_u[...] = jnp.zeros_like(acc_u)

        @pl.when(i == at_f + n_k + 3)
        def _():
            relay_keys(0)

    finish_keys(1)
    place_keys(0)
    own_ref[...] = kbuf[:, r].reshape(total_rows, hidden).T
    relay_keys(1)
    place_keys(1)

    @pl.loop(0, n_j)
    def _(j):
        for pos in remote:
            a_copy(j, pos).wait_send()

        @pl.when(j >= n_k)
        def _():
            a_copy(j, 0).wait_send()

        x_copy(j).wait_send()
        s_copy(j).wait_send()
        f_copy(j).wait_send()

    for p in range(pieces):
        key_copy(p, r, across, 0).wait_send()
        key_copy(p, r, sib, 1).wait_send()
        key_copy(p, across, sib, 2).wait_send()


def gram_kernel(factor, own_ref, keys_ref, out_ref):
    out_ref[...] = jnp.dot(
        own_ref[...], keys_ref[...], preferred_element_type=jnp.float32) * factor


def body(tokens, routes, counts, w_gate, w_up):
    n_e = lax.axis_size("expert")
    n_r = lax.axis_size("replica")
    n_tok, width = tokens.shape
    hidden = w_gate.shape[2]
    cap = n_tok * TOP // N_ROUTED
    n_k = 7
    kc = width // n_k
    pieces = 4
    total = n_e * n_r * cap
    sizes = (n_e, n_r, cap, n_tok, n_k, kc, pieces)
    bf = jnp.bfloat16
    dma = pltpu.SemaphoreType.DMA
    vmem = pl.BlockSpec(memory_space=pltpu.VMEM)
    hbm = pl.BlockSpec(memory_space=pl.ANY)
    keys, own = pl.pallas_call(
        functools.partial(exchange_kernel, sizes),
        out_shape=(
            jax.ShapeDtypeStruct((total, n_r * hidden), bf),
            jax.ShapeDtypeStruct((hidden, total), bf),
        ),
        in_specs=[pl.BlockSpec(memory_space=pltpu.SMEM), vmem, hbm, hbm, hbm],
        out_specs=(vmem, vmem),
        scratch_shapes=[
            pltpu.VMEM((n_k, n_tok, kc), bf),
            pltpu.VMEM((n_k, kc, hidden), bf),
            pltpu.VMEM((n_k, kc, hidden), bf),
            pltpu.VMEM((n_k, n_e, cap, kc), bf),
            pltpu.VMEM((2 * n_k, n_r, n_e // 2, cap, kc), bf),
            pltpu.VMEM((total // 2, hidden), jnp.float32),
            pltpu.VMEM((total // 2, hidden), jnp.float32),
            pltpu.VMEM((pieces, n_r, total // pieces, hidden), bf),
            dma((n_k,)), dma((n_k,)), dma((n_k,)),
            dma((2 * n_k, n_e // 2)), dma((2 * n_k, n_e // 2)),
            dma((2 * n_k,)), dma((2 * n_k,)), dma((2 * n_k,)),
            dma((2 * n_k,)), dma((2 * n_k,)), dma((2 * n_k,)),
            dma((3, pieces)), dma((3, pieces)),
        ],
        compiler_params=pltpu.CompilerParams(
            collective_id=0, has_side_effects=True, vmem_limit_bytes=60 * 1024 * 1024),
        cost_estimate=pl.CostEstimate(
            flops=4 * total * width * hidden,
            bytes_accessed=4 * width * hidden + 2 * n_tok * width,
            transcendentals=total * hidden),
    )(counts, routes.T, tokens, w_gate, w_up)
    factor = 1.0 / (n_e * cap)
    gram = pl.pallas_call(
        functools.partial(gram_kernel, factor),
        grid=(n_r,),
        out_shape=jax.ShapeDtypeStruct((hidden, n_r * hidden), jnp.float32),
        in_specs=[
            pl.BlockSpec((hidden, total), lambda c: (0, 0)),
            pl.BlockSpec((total, hidden), lambda c: (0, c)),
        ],
        out_specs=pl.BlockSpec((hidden, hidden), lambda c: (0, c)),
        compiler_params=pltpu.CompilerParams(vmem_limit_bytes=32 * 1024 * 1024),
        cost_estimate=pl.CostEstimate(
            flops=2 * total * hidden * hidden * n_r,
            bytes_accessed=4 * n_r * hidden * hidden + 2 * total * hidden * (n_r + 1),
            transcendentals=0),
    )(own, keys)
    return gram[None]


def solution(mesh):
    return jax.shard_map(
        body,
        mesh=mesh,
        in_specs=(
            P(("expert", "replica"), None),
            P(("expert", "replica"), None),
            P(("expert", "replica")),
            P("expert", None, "replica"),
            P("expert", None, "replica"),
        ),
        out_specs=P("expert", "replica", None),
        check_vma=False,
    )
```

```python
import functools

import jax
import jax.numpy as jnp
from jax import lax
from jax.experimental import pallas as pl
from jax.experimental.pallas import tpu as pltpu
from jax.sharding import PartitionSpec as P

N_ROUTED = 256
TOP = 8
MESH = pl.DeviceIdType.MESH


def exchange_kernel(
    sizes, counts_ref, routes_ref, tokens_hbm, gate_hbm, up_hbm, keys_ref, own_ref,
    tok, wg, wu, slots, rows, acc_g, acc_u, kbuf,
    tok_sem, wg_sem, wu_sem, a_send, a_recv, x_send, x_recv, s_send, s_recv,
    f_send, f_recv, k_send, k_recv, l_send, l_recv,
):
    n_e, n_r, cap, n_tok, n_k, kc, pieces = sizes
    total_rows = n_e * n_r * cap
    piece = total_rows // pieces
    half_rows = total_rows // 2
    half = n_e // 2
    n_j = 2 * n_k
    hidden = acc_g.shape[1]
    e = lax.axis_index("expert")
    r = lax.axis_index("replica")
    sib = r + 1 - 2 * (r % 2)
    across = (r + 2) % n_r

    def tok_copy(k):
        return pltpu.make_async_copy(
            tokens_hbm.at[:, pl.ds(k * kc, kc)], tok.at[k], tok_sem.at[k])

    def w_copy(hbm, buf, sem, k):
        return pltpu.make_async_copy(hbm.at[0, pl.ds(k * kc, kc), :], buf.at[k], sem.at[k])

    barrier = pltpu.get_barrier_semaphore()
    for s in range(1, n_e):
        pl.semaphore_signal(barrier, inc=1, device_id=((e + s) % n_e, r), device_id_type=MESH)
    pl.semaphore_signal(barrier, inc=1, device_id=(e, sib), device_id_type=MESH)
    pl.semaphore_signal(barrier, inc=1, device_id=(e, across), device_id_type=MESH)

    for k in range(n_k):
        tok_copy(k).start()

    n_s = n_e * cap
    count = counts_ref[0]
    slot = lax.broadcasted_iota(jnp.int32, (n_s, n_tok), 0)
    token = lax.broadcasted_iota(jnp.int32, (n_s, n_tok), 1)
    slot_expert = slot // cap
    hit = routes_ref[0:1, :] == slot_expert
    for c in range(1, TOP):
        hit = hit | (routes_ref[c:c + 1, :] == slot_expert)
    hit = hit & (token < count)
    before = lax.broadcasted_iota(jnp.int32, (n_tok, n_tok), 0) < lax.broadcasted_iota(
        jnp.int32, (n_tok, n_tok), 1)
    hit_f = jnp.where(hit, 1.0, 0.0)
    rank = jnp.dot(
        hit_f.astype(jnp.bfloat16), jnp.where(before, 1.0, 0.0).astype(jnp.bfloat16),
        preferred_element_type=jnp.float32)
    place = (slot % cap).astype(jnp.float32)
    choice = jnp.where(rank == place, hit_f, 0.0).astype(jnp.bfloat16)

    acc_g[...] = jnp.zeros_like(acc_g)
    acc_u[...] = jnp.zeros_like(acc_u)

    pl.semaphore_wait(barrier, n_e + 1)

    def a_copy(j, pos):
        to = (e + 2 * pos + j // n_k) % n_e
        return pltpu.make_async_remote_copy(
            src_ref=slots.at[j % n_k, to], dst_ref=rows.at[j, r, pos],
            send_sem=a_send.at[j, pos], recv_sem=a_recv.at[j, pos],
            device_id=(to, r), device_id_type=MESH)

    def row_copy(k, who, to, send, recv):
        return pltpu.make_async_remote_copy(
            src_ref=rows.at[k, who], dst_ref=rows.at[k, who],
            send_sem=send.at[k], recv_sem=recv.at[k],
            device_id=(e, to), device_id_type=MESH)

    def x_copy(k):
        return row_copy(k, r, across, x_send, x_recv)

    def l_copy(k):
        return pltpu.make_async_remote_copy(
            src_ref=rows.at[k, r, 0], dst_ref=rows.at[k, r, 0],
            send_sem=l_send.at[k], recv_sem=l_recv.at[k],
            device_id=(e, across), device_id_type=MESH)

    def y_copy(k):
        return pltpu.make_async_remote_copy(
            src_ref=rows.at[k, r, pl.ds(1, half - 1)], dst_ref=rows.at[k, r, pl.ds(1, half - 1)],
            send_sem=x_send.at[k], recv_sem=x_recv.at[k],
            device_id=(e, across), device_id_type=MESH)

    def s_copy(k):
        return row_copy(k, r, sib, s_send, s_recv)

    def f_copy(k):
        return row_copy(k, across, sib, f_send, f_recv)

    order = sorted(range(half), key=lambda pos: abs(2 * pos - half))
    remote = [pos for pos in order if pos > 0]

    def key_copy(p, who, to, n):
        return pltpu.make_async_remote_copy(
            src_ref=kbuf.at[p, who], dst_ref=kbuf.at[p, who],
            send_sem=k_send.at[n, p], recv_sem=k_recv.at[n, p],
            device_id=(e, to), device_id_type=MESH)

    def finish_keys(h):
        for q in range(pieces // 2):
            p = h * (pieces // 2) + q
            g = acc_g[q * piece:(q + 1) * piece, :]
            u = acc_u[q * piece:(q + 1) * piece, :]
            kbuf[p, r] = ((g / (1.0 + jnp.exp(-g))) * u).astype(jnp.bfloat16)
            key_copy(p, r, across, 0).start()
            key_copy(p, r, sib, 1).start()

    def relay_keys(h):
        for q in range(pieces // 2):
            p = h * (pieces // 2) + q
            key_copy(p, r, across, 0).wait_recv()
            key_copy(p, across, sib, 2).start()

    def place_keys(h):
        for q in range(pieces // 2):
            p = h * (pieces // 2) + q
            key_copy(p, r, sib, 1).wait_recv()
            key_copy(p, across, sib, 2).wait_recv()
            for o in range(n_r):
                keys_ref[p * piece:(p + 1) * piece, o * hidden:(o + 1) * hidden] = kbuf[p, o]

    groups = max(1, half_rows // 256)
    per = n_r // groups
    step_rows = half_rows // groups
    ahead, lag_x, lag_f = 3, 2, 1
    at_x = ahead + lag_x
    at_f = at_x + lag_f

    @pl.loop(0, n_j + at_f)
    def _(i):
        @pl.when(i < n_k)
        def _():
            tok_copy(i).wait()
            picked = jnp.dot(choice, tok[i], preferred_element_type=jnp.float32)
            slots[i] = picked.reshape(n_e, cap, kc).astype(jnp.bfloat16)
            for pos in remote:
                a_copy(i, pos).start()
            rows[i, r, 0] = slots[i, e]
            l_copy(i).start()
            w_copy(gate_hbm, wg, wg_sem, i).start()
            w_copy(up_hbm, wu, wu_sem, i).start()

        @pl.when((i >= n_k) & (i < n_j))
        def _():
            for pos in order:
                a_copy(i, pos).start()

        @pl.when((i >= ahead) & (i < n_j + ahead))
        def _():
            j = i - ahead
            for pos in remote:
                a_copy(j, pos).wait_recv()

            @pl.when(j >= n_k)
            def _():
                a_copy(j, 0).wait_recv()
                x_copy(j).start()

            @pl.when(j < n_k)
            def _():
                y_copy(j).start()

            s_copy(j).start()

        @pl.when((i >= at_x) & (i < n_j + at_x))
        def _():
            j = i - at_x

            @pl.when(j < n_k)
            def _():
                l_copy(j).wait_recv()
                y_copy(j).wait_recv()

            @pl.when(j >= n_k)
            def _():
                x_copy(j).wait_recv()

            f_copy(j).start()

        @pl.when(i >= at_f)
        def _():
            j = i - at_f
            k = j % n_k

            @pl.when(j < n_k)
            def _():
                w_copy(gate_hbm, wg, wg_sem, k).wait()
                w_copy(up_hbm, wu, wu_sem, k).wait()

            s_copy(j).wait_recv()
            f_copy(j).wait_recv()
            for g in range(groups):
                block = rows[j, g * per:(g + 1) * per].reshape(step_rows, kc)
                at = slice(g * step_rows, (g + 1) * step_rows)
                acc_g[at, :] += jnp.dot(block, wg[k], preferred_element_type=jnp.float32)
                acc_u[at, :] += jnp.dot(block, wu[k], preferred_element_type=jnp.float32)

        @pl.when(i == at_f + n_k - 1)
        def _():
            finish_keys(0)
            acc_g[...] = jnp.zeros_like(acc_g)
            acc_u[...] = jnp.zeros_like(acc_u)

        @pl.when(i == at_f + n_k + 3)
        def _():
            relay_keys(0)

    finish_keys(1)
    place_keys(0)
    own_ref[...] = kbuf[:, r].reshape(total_rows, hidden).T
    relay_keys(1)
    place_keys(1)

    @pl.loop(0, n_j)
    def _(j):
        for pos in remote:
            a_copy(j, pos).wait_send()

        @pl.when(j >= n_k)
        def _():
            a_copy(j, 0).wait_send()
            x_copy(j).wait_send()

        @pl.when(j < n_k)
        def _():
            l_copy(j).wait_send()
            y_copy(j).wait_send()

        s_copy(j).wait_send()
        f_copy(j).wait_send()

    for p in range(pieces):
        key_copy(p, r, across, 0).wait_send()
        key_copy(p, r, sib, 1).wait_send()
        key_copy(p, across, sib, 2).wait_send()


def gram_kernel(factor, own_ref, keys_ref, out_ref):
    out_ref[...] = jnp.dot(
        own_ref[...], keys_ref[...], preferred_element_type=jnp.float32) * factor


def body(tokens, routes, counts, w_gate, w_up):
    n_e = lax.axis_size("expert")
    n_r = lax.axis_size("replica")
    n_tok, width = tokens.shape
    hidden = w_gate.shape[2]
    cap = n_tok * TOP // N_ROUTED
    n_k = 7
    kc = width // n_k
    pieces = 4
    total = n_e * n_r * cap
    sizes = (n_e, n_r, cap, n_tok, n_k, kc, pieces)
    bf = jnp.bfloat16
    dma = pltpu.SemaphoreType.DMA
    vmem = pl.BlockSpec(memory_space=pltpu.VMEM)
    hbm = pl.BlockSpec(memory_space=pl.ANY)
    keys, own = pl.pallas_call(
        functools.partial(exchange_kernel, sizes),
        out_shape=(
            jax.ShapeDtypeStruct((total, n_r * hidden), bf),
            jax.ShapeDtypeStruct((hidden, total), bf),
        ),
        in_specs=[pl.BlockSpec(memory_space=pltpu.SMEM), vmem, hbm, hbm, hbm],
        out_specs=(vmem, vmem),
        scratch_shapes=[
            pltpu.VMEM((n_k, n_tok, kc), bf),
            pltpu.VMEM((n_k, kc, hidden), bf),
            pltpu.VMEM((n_k, kc, hidden), bf),
            pltpu.VMEM((n_k, n_e, cap, kc), bf),
            pltpu.VMEM((2 * n_k, n_r, n_e // 2, cap, kc), bf),
            pltpu.VMEM((total // 2, hidden), jnp.float32),
            pltpu.VMEM((total // 2, hidden), jnp.float32),
            pltpu.VMEM((pieces, n_r, total // pieces, hidden), bf),
            dma((n_k,)), dma((n_k,)), dma((n_k,)),
            dma((2 * n_k, n_e // 2)), dma((2 * n_k, n_e // 2)),
            dma((2 * n_k,)), dma((2 * n_k,)), dma((2 * n_k,)),
            dma((2 * n_k,)), dma((2 * n_k,)), dma((2 * n_k,)),
            dma((3, pieces)), dma((3, pieces)), dma((n_k,)), dma((n_k,)),
        ],
        compiler_params=pltpu.CompilerParams(
            collective_id=0, has_side_effects=True, vmem_limit_bytes=60 * 1024 * 1024),
        cost_estimate=pl.CostEstimate(
            flops=4 * total * width * hidden,
            bytes_accessed=4 * width * hidden + 2 * n_tok * width,
            transcendentals=total * hidden),
    )(counts, routes.T, tokens, w_gate, w_up)
    factor = 1.0 / (n_e * cap)
    gram = pl.pallas_call(
        functools.partial(gram_kernel, factor),
        grid=(n_r,),
        out_shape=jax.ShapeDtypeStruct((hidden, n_r * hidden), jnp.float32),
        in_specs=[
            pl.BlockSpec((hidden, total), lambda c: (0, 0)),
            pl.BlockSpec((total, hidden), lambda c: (0, c)),
        ],
        out_specs=pl.BlockSpec((hidden, hidden), lambda c: (0, c)),
        compiler_params=pltpu.CompilerParams(vmem_limit_bytes=60 * 1024 * 1024),
        cost_estimate=pl.CostEstimate(
            flops=2 * total * hidden * hidden * n_r,
            bytes_accessed=4 * n_r * hidden * hidden + 2 * total * hidden * (n_r + 1),
            transcendentals=0),
    )(own, keys)
    return gram[None]


def solution(mesh):
    return jax.shard_map(
        body,
        mesh=mesh,
        in_specs=(
            P(("expert", "replica"), None),
            P(("expert", "replica"), None),
            P(("expert", "replica")),
            P("expert", None, "replica"),
            P("expert", None, "replica"),
        ),
        out_specs=P("expert", "replica", None),
        check_vma=False,
    )
```

```python
import functools

import jax
import jax.numpy as jnp
from jax import lax
from jax.experimental import pallas as pl
from jax.experimental.pallas import tpu as pltpu
from jax.sharding import PartitionSpec as P

N_ROUTED = 256
TOP = 8
MESH = pl.DeviceIdType.MESH


def exchange_kernel(
    sizes, counts_ref, routes_ref, tokens_hbm, gate_hbm, up_hbm, keys_ref, own_ref,
    tok, wg, wu, slots, rows, acc_g, acc_u, kbuf,
    tok_sem, wg_sem, wu_sem, a_send, a_recv, x_send, x_recv, s_send, s_recv,
    f_send, f_recv, k_send, k_recv, l_send, l_recv,
):
    n_e, n_r, cap, n_tok, n_k, kc, pieces = sizes
    total_rows = n_e * n_r * cap
    piece = total_rows // pieces
    half_rows = total_rows // 2
    half = n_e // 2
    n_j = 2 * n_k
    hidden = acc_g.shape[1]
    e = lax.axis_index("expert")
    r = lax.axis_index("replica")
    sib = r + 1 - 2 * (r % 2)
    across = (r + 2) % n_r

    def tok_copy(k):
        return pltpu.make_async_copy(
            tokens_hbm.at[:, pl.ds(k * kc, kc)], tok.at[k], tok_sem.at[k])

    def w_copy(hbm, buf, sem, k):
        return pltpu.make_async_copy(hbm.at[0, pl.ds(k * kc, kc), :], buf.at[k], sem.at[k])

    barrier = pltpu.get_barrier_semaphore()
    for s in range(1, n_e):
        pl.semaphore_signal(barrier, inc=1, device_id=((e + s) % n_e, r), device_id_type=MESH)
    pl.semaphore_signal(barrier, inc=1, device_id=(e, sib), device_id_type=MESH)
    pl.semaphore_signal(barrier, inc=1, device_id=(e, across), device_id_type=MESH)

    for k in range(n_k):
        tok_copy(k).start()

    n_s = n_e * cap
    count = counts_ref[0]
    slot = lax.broadcasted_iota(jnp.int32, (n_s, n_tok), 0)
    token = lax.broadcasted_iota(jnp.int32, (n_s, n_tok), 1)
    slot_expert = slot // cap
    hit = routes_ref[0:1, :] == slot_expert
    for c in range(1, TOP):
        hit = hit | (routes_ref[c:c + 1, :] == slot_expert)
    hit = hit & (token < count)
    before = lax.broadcasted_iota(jnp.int32, (n_tok, n_tok), 0) < lax.broadcasted_iota(
        jnp.int32, (n_tok, n_tok), 1)
    hit_f = jnp.where(hit, 1.0, 0.0)
    rank = jnp.dot(
        hit_f.astype(jnp.bfloat16), jnp.where(before, 1.0, 0.0).astype(jnp.bfloat16),
        preferred_element_type=jnp.float32)
    place = (slot % cap).astype(jnp.float32)
    choice = jnp.where(rank == place, hit_f, 0.0).astype(jnp.bfloat16)

    acc_g[...] = jnp.zeros_like(acc_g)
    acc_u[...] = jnp.zeros_like(acc_u)

    pl.semaphore_wait(barrier, n_e + 1)

    def a_copy(j, pos):
        to = (e + 2 * pos + j // n_k) % n_e
        return pltpu.make_async_remote_copy(
            src_ref=slots.at[j % n_k, to], dst_ref=rows.at[j, r, pos],
            send_sem=a_send.at[j, pos], recv_sem=a_recv.at[j, pos],
            device_id=(to, r), device_id_type=MESH)

    def row_copy(k, who, to, send, recv):
        return pltpu.make_async_remote_copy(
            src_ref=rows.at[k, who], dst_ref=rows.at[k, who],
            send_sem=send.at[k], recv_sem=recv.at[k],
            device_id=(e, to), device_id_type=MESH)

    def x_copy(k):
        return row_copy(k, r, across, x_send, x_recv)

    def l_copy(k):
        return pltpu.make_async_remote_copy(
            src_ref=rows.at[k, r, 0], dst_ref=rows.at[k, r, 0],
            send_sem=l_send.at[k], recv_sem=l_recv.at[k],
            device_id=(e, across), device_id_type=MESH)

    def y_copy(k):
        return pltpu.make_async_remote_copy(
            src_ref=rows.at[k, r, pl.ds(1, half - 1)], dst_ref=rows.at[k, r, pl.ds(1, half - 1)],
            send_sem=x_send.at[k], recv_sem=x_recv.at[k],
            device_id=(e, across), device_id_type=MESH)

    def s_copy(k):
        return row_copy(k, r, sib, s_send, s_recv)

    def f_copy(k):
        return row_copy(k, across, sib, f_send, f_recv)

    order = sorted(range(half), key=lambda pos: abs(2 * pos - half))
    remote = [pos for pos in order if pos > 0]

    def key_copy(p, who, to, n):
        return pltpu.make_async_remote_copy(
            src_ref=kbuf.at[p, who], dst_ref=kbuf.at[p, who],
            send_sem=k_send.at[n, p], recv_sem=k_recv.at[n, p],
            device_id=(e, to), device_id_type=MESH)

    def finish_keys(h):
        for q in range(pieces // 2):
            p = h * (pieces // 2) + q
            g = acc_g[q * piece:(q + 1) * piece, :]
            u = acc_u[q * piece:(q + 1) * piece, :]
            kbuf[p, r] = ((g / (1.0 + jnp.exp(-g))) * u).astype(jnp.bfloat16)
            key_copy(p, r, across, 0).start()
            key_copy(p, r, sib, 1).start()

    def relay_keys(h):
        for q in range(pieces // 2):
            p = h * (pieces // 2) + q
            key_copy(p, r, across, 0).wait_recv()
            key_copy(p, across, sib, 2).start()

    def place_keys(h):
        for q in range(pieces // 2):
            p = h * (pieces // 2) + q
            key_copy(p, r, sib, 1).wait_recv()
            key_copy(p, across, sib, 2).wait_recv()
            for o in range(n_r):
                keys_ref[p * piece:(p + 1) * piece, o * hidden:(o + 1) * hidden] = kbuf[p, o]

    groups = max(1, half_rows // 256)
    per = n_r // groups
    step_rows = half_rows // groups
    ahead, lag_x, lag_f = 3, 2, 1
    at_x = ahead + lag_x
    at_f = at_x + lag_f

    @pl.loop(0, n_j + at_f)
    def _(i):
        @pl.when(i < n_k)
        def _():
            tok_copy(i).wait()
            picked = jnp.dot(choice, tok[i], preferred_element_type=jnp.float32)
            slots[i] = picked.reshape(n_e, cap, kc).astype(jnp.bfloat16)
            for pos in remote:
                a_copy(i, pos).start()
            rows[i, r, 0] = slots[i, e]
            l_copy(i).start()
            w_copy(gate_hbm, wg, wg_sem, i).start()
            w_copy(up_hbm, wu, wu_sem, i).start()

        @pl.when((i >= n_k) & (i < n_j))
        def _():
            for pos in order:
                a_copy(i, pos).start()

        @pl.when((i >= ahead) & (i < n_j + ahead))
        def _():
            j = i - ahead
            for pos in remote:
                a_copy(j, pos).wait_recv()

            @pl.when(j >= n_k)
            def _():
                a_copy(j, 0).wait_recv()
                x_copy(j).start()

            @pl.when(j < n_k)
            def _():
                y_copy(j).start()

            s_copy(j).start()

        @pl.when((i >= at_x) & (i < n_j + at_x))
        def _():
            j = i - at_x

            @pl.when(j < n_k)
            def _():
                l_copy(j).wait_recv()
                y_copy(j).wait_recv()

            @pl.when(j >= n_k)
            def _():
                x_copy(j).wait_recv()

            f_copy(j).start()

        @pl.when(i >= at_f)
        def _():
            j = i - at_f
            k = j % n_k

            @pl.when(j < n_k)
            def _():
                w_copy(gate_hbm, wg, wg_sem, k).wait()
                w_copy(up_hbm, wu, wu_sem, k).wait()

            s_copy(j).wait_recv()
            f_copy(j).wait_recv()
            for g in range(groups):
                block = rows[j, g * per:(g + 1) * per].reshape(step_rows, kc)
                at = slice(g * step_rows, (g + 1) * step_rows)
                acc_g[at, :] += jnp.dot(block, wg[k], preferred_element_type=jnp.float32)
                acc_u[at, :] += jnp.dot(block, wu[k], preferred_element_type=jnp.float32)

        @pl.when(i == at_f + n_k - 1)
        def _():
            finish_keys(0)
            acc_g[...] = jnp.zeros_like(acc_g)
            acc_u[...] = jnp.zeros_like(acc_u)

        @pl.when(i == at_f + n_k + 3)
        def _():
            relay_keys(0)

    finish_keys(1)
    place_keys(0)
    own_ref[...] = kbuf[:, r].reshape(total_rows, hidden).T
    relay_keys(1)
    place_keys(1)

    @pl.loop(0, n_j)
    def _(j):
        for pos in remote:
            a_copy(j, pos).wait_send()

        @pl.when(j >= n_k)
        def _():
            a_copy(j, 0).wait_send()
            x_copy(j).wait_send()

        @pl.when(j < n_k)
        def _():
            l_copy(j).wait_send()
            y_copy(j).wait_send()

        s_copy(j).wait_send()
        f_copy(j).wait_send()

    for p in range(pieces):
        key_copy(p, r, across, 0).wait_send()
        key_copy(p, r, sib, 1).wait_send()
        key_copy(p, across, sib, 2).wait_send()


def gram_kernel(factor, own_ref, keys_ref, out_ref):
    out_ref[...] = jnp.dot(
        own_ref[...], keys_ref[...], preferred_element_type=jnp.float32) * factor


def body(tokens, routes, counts, w_gate, w_up):
    n_e = lax.axis_size("expert")
    n_r = lax.axis_size("replica")
    n_tok, width = tokens.shape
    hidden = w_gate.shape[2]
    cap = n_tok * TOP // N_ROUTED
    n_k = 7
    kc = width // n_k
    pieces = 4
    total = n_e * n_r * cap
    sizes = (n_e, n_r, cap, n_tok, n_k, kc, pieces)
    bf = jnp.bfloat16
    dma = pltpu.SemaphoreType.DMA
    vmem = pl.BlockSpec(memory_space=pltpu.VMEM)
    hbm = pl.BlockSpec(memory_space=pl.ANY)
    keys, own = pl.pallas_call(
        functools.partial(exchange_kernel, sizes),
        out_shape=(
            jax.ShapeDtypeStruct((total, n_r * hidden), bf),
            jax.ShapeDtypeStruct((hidden, total), bf),
        ),
        in_specs=[pl.BlockSpec(memory_space=pltpu.SMEM), vmem, hbm, hbm, hbm],
        out_specs=(vmem, vmem),
        scratch_shapes=[
            pltpu.VMEM((n_k, n_tok, kc), bf),
            pltpu.VMEM((n_k, kc, hidden), bf),
            pltpu.VMEM((n_k, kc, hidden), bf),
            pltpu.VMEM((n_k, n_e, cap, kc), bf),
            pltpu.VMEM((2 * n_k, n_r, n_e // 2, cap, kc), bf),
            pltpu.VMEM((total // 2, hidden), jnp.float32),
            pltpu.VMEM((total // 2, hidden), jnp.float32),
            pltpu.VMEM((pieces, n_r, total // pieces, hidden), bf),
            dma((n_k,)), dma((n_k,)), dma((n_k,)),
            dma((2 * n_k, n_e // 2)), dma((2 * n_k, n_e // 2)),
            dma((2 * n_k,)), dma((2 * n_k,)), dma((2 * n_k,)),
            dma((2 * n_k,)), dma((2 * n_k,)), dma((2 * n_k,)),
            dma((3, pieces)), dma((3, pieces)), dma((n_k,)), dma((n_k,)),
        ],
        compiler_params=pltpu.CompilerParams(
            collective_id=0, has_side_effects=True, vmem_limit_bytes=60 * 1024 * 1024),
        cost_estimate=pl.CostEstimate(
            flops=4 * total * width * hidden,
            bytes_accessed=4 * width * hidden + 2 * n_tok * width,
            transcendentals=total * hidden),
    )(counts, routes.T, tokens, w_gate, w_up)
    factor = 1.0 / (n_e * cap)
    gram = pl.pallas_call(
        functools.partial(gram_kernel, factor),
        grid=(2 * n_r,),
        out_shape=jax.ShapeDtypeStruct((hidden, n_r * hidden), jnp.float32),
        in_specs=[
            pl.BlockSpec((hidden, total), lambda c: (0, 0)),
            pl.BlockSpec((total, hidden // 2), lambda c: (0, c)),
        ],
        out_specs=pl.BlockSpec((hidden, hidden // 2), lambda c: (0, c)),
        compiler_params=pltpu.CompilerParams(vmem_limit_bytes=60 * 1024 * 1024),
        cost_estimate=pl.CostEstimate(
            flops=2 * total * hidden * hidden * n_r,
            bytes_accessed=4 * n_r * hidden * hidden + 2 * total * hidden * (n_r + 1),
            transcendentals=0),
    )(own, keys)
    return gram[None]


def solution(mesh):
    return jax.shard_map(
        body,
        mesh=mesh,
        in_specs=(
            P(("expert", "replica"), None),
            P(("expert", "replica"), None),
            P(("expert", "replica")),
            P("expert", None, "replica"),
            P("expert", None, "replica"),
        ),
        out_specs=P("expert", "replica", None),
        check_vma=False,
    )
```
